32 devices in a mesh: tick: 16 (over z, y, x), wire: 2 (over core).
Axes of the slice: x: 2, y: 2, z: 4, core: 2. Of those that a mesh axis runs over, the one named last changes fastest.
Arguments:
- trigger: bfloat16 [2048, 16, 1280], P('tick', None, 'wire'), may hold values from -6 to 6
- response: float32 [2, 21, 1024], replicated, may hold values from -1.2 to 1.2
- wiener: float32 [1024], replicated, may hold values from 0.2 to 2
- roi_mask: int32 [16, 1280, 16], P('tick', 'wire'), may hold values 0 or 1
- cell_map: int32 [16, 1280], P('tick', 'wire'), may hold values from 0 to 127, as said below
Outputs:
- signal: bfloat16 [16, 1280, 2048], P('tick', 'wire')
- cell_charge: float32 [128, 2048], P('tick', 'wire')
The draws below stay inside these ranges and needn't reach their ends.
Inputs may be any that keep to these rules, and one draw needn't show every extreme that they name: `cell_map`: A channel's cell c belongs to owner c // 8. Among the 640 channels of one device (an aligned block of 640 wires of one plane), at most 80 name cells of one owner; in every draw some owner gets exactly 80 channels from every such block.
All inputs are finite; a program needn't handle non-finite values. No bound on the sum of `roi_mask` on one device may be relied on, other than what follows from the above.
Results may differ from the reference program's by a relative error of at most 0.008.
Values may be sent and summed in bfloat16 or wider, within the bound.
A program may use at most 128 MiB of HBM per device.

```python
import math
import jax
import jax.numpy as jnp
from jax import lax

TICKS = 2048
WIRES = 1280
RESP_TAPS = 21
ROI_TICKS = 128
CELLS_OWN = 8
FREQS = 1024
HALO = 10
WIRE_DEV = 640
PLANES = 16
ROI_BLOCKS = 16
CAP = 80
CELLS = 128
N_TICK = 16


def draw_cell_map(key, part):
    hot_key, block_key = jax.random.split(jax.random.fold_in(key, 17))
    hot_owner = jax.random.randint(hot_key, (), 0, N_TICK, dtype=jnp.int32)
    block_count = PLANES * WIRES // WIRE_DEV

    def draw_block(block_seed):
        slot_key, order_key, cell_key = jax.random.split(block_seed, 3)
        slots = jax.random.permutation(slot_key, (N_TICK - 1) * CAP)
        chosen = slots[:WIRE_DEV - CAP].astype(jnp.int32)
        others = chosen // CAP
        others = others + (others >= hot_owner).astype(jnp.int32)
        owners = jnp.concatenate([jnp.full((CAP,), hot_owner, jnp.int32), others])
        owners = jax.random.permutation(order_key, owners)
        cells = jax.random.randint(cell_key, (WIRE_DEV,), 0, CELLS_OWN, dtype=jnp.int32)
        return owners * CELLS_OWN + cells
    block_keys = jax.random.split(block_key, block_count)
    return jax.vmap(draw_block)(block_keys).reshape(PLANES, WIRES)


def touch_ends(values, rng, least, largest):
    dims = values.shape
    index_at = [jax.random.randint(jax.random.fold_in(rng, axis), (), 0, dims[axis]) for axis in range(len(dims))]
    values = values.at[tuple(index_at)].set(least)
    longest = dims.index(max(dims))
    index_at[longest] = (index_at[longest] + 1) % dims[longest]
    return values.at[tuple(index_at)].set(largest)


def shard_levels(key, shape, pieces, smallest, high):
    gain = 1.0
    for axis_at, parts in pieces:
        heights = jax.random.uniform(jax.random.fold_in(jax.random.fold_in(key, 6), axis_at), (parts,), jnp.float32, smallest / len(pieces), high / len(pieces))
        gain = gain * jnp.repeat(jnp.exp(heights), shape[axis_at] // parts).reshape((-1,) + (1,) * (len(shape) - 1 - axis_at))
    return gain


def noise(stream_key, dims, width, most, cuts=(), kind=jnp.bfloat16):
    result = jax.random.normal(stream_key, dims, jnp.float32) * width
    if len(cuts) > 0:
        result = shard_levels(stream_key, dims, cuts, -0.22, 0.18) * result
    return jnp.clip(result, min=-most, max=most).astype(kind)


def setup_inputs(seed: int = 0) -> dict:
    key_of = jax.random.split(jax.random.key(seed), 6)
    trigger = noise(key_of[0], (TICKS, PLANES, WIRES), 1.0, 6.0, ((0, 16), (2, 2)))
    response = noise(key_of[1], (2, RESP_TAPS, FREQS), 0.2, 1.2, (), jnp.float32)
    wiener = jnp.clip(jnp.exp(jax.random.uniform(key_of[2], (FREQS,), jnp.float32, math.log(0.2), math.log(2.0))), 0.2, 2.0)
    roi_mask = touch_ends((jax.random.randint(key_of[3], (PLANES, WIRES, ROI_BLOCKS), 0, 4) < 3).astype(jnp.int32), jax.random.fold_in(key_of[3], 1), 0, 1)
    cell_map = draw_cell_map(jax.random.fold_in(key_of[5], 71), 0)
    return dict(trigger=trigger, response=response, wiener=wiener, roi_mask=roi_mask, cell_map=cell_map)


charge_scale = 0.1


def build_tables():
    frequency = jnp.arange(FREQS, dtype=jnp.int32)
    tick_index = jnp.arange(TICKS, dtype=jnp.int32)
    phase_angle = ((frequency[:, None] * tick_index[None, :]) % TICKS).astype(jnp.float32) * (2.0 * math.pi / TICKS)
    cosine = jnp.cos(phase_angle).astype(jnp.bfloat16)
    sine_table = jnp.sin(phase_angle).astype(jnp.bfloat16)
    forward = jnp.concatenate([cosine, -sine_table], axis=0)
    weight = jnp.where(frequency == 0, 1.0, 2.0).astype(jnp.bfloat16)[:, None]
    inverse = jnp.concatenate([cosine * weight, -sine_table * weight], axis=0)
    return forward, inverse


def deconvolve(spectrum, response, wiener, wire_count):
    real_part = spectrum[:FREQS].astype(jnp.float32)
    imag_part = spectrum[FREQS:].astype(jnp.float32)
    sum_real = jnp.zeros((FREQS, wire_count), jnp.float32)
    sum_imag = jnp.zeros((FREQS, wire_count), jnp.float32)
    for offset in range(RESP_TAPS):
        shifted_real = real_part[:, offset:offset + wire_count]
        shifted_imag = imag_part[:, offset:offset + wire_count]
        resp_real = response[0, offset][:, None]
        resp_imag = response[1, offset][:, None]
        sum_real = sum_real + resp_real * shifted_real - resp_imag * shifted_imag
        sum_imag = sum_imag + resp_real * shifted_imag + resp_imag * shifted_real
    gain_column = wiener[:, None]
    return jnp.concatenate([sum_real * gain_column, sum_imag * gain_column], axis=0).astype(jnp.bfloat16)


def reference(trigger, response, wiener, roi_mask, cell_map):
    forward, inverse = build_tables()
    norm_factor = TICKS ** -0.5
    waves = jnp.moveaxis(trigger, 1, 0)

    def one_plane(inputs):
        plane_waves, plane_mask = inputs
        spectrum = (jnp.dot(forward, plane_waves, preferred_element_type=jnp.float32) * norm_factor).astype(jnp.bfloat16)
        extended = jnp.pad(spectrum, ((0, 0), (HALO, HALO)))
        filtered = deconvolve(extended, response, wiener, WIRES)
        unmasked = lax.dot_general(filtered, inverse, (((0,), (0,)), ((), ())), preferred_element_type=jnp.float32) * norm_factor
        blocks = plane_mask.astype(jnp.float32)
        return (unmasked.reshape(WIRES, ROI_BLOCKS, ROI_TICKS) * blocks[:, :, None]).reshape(WIRES, TICKS).astype(jnp.bfloat16)

    signal = lax.map(one_plane, (waves, roi_mask))

    def collect(total, inputs):
        plane_signal, plane_cells = inputs
        return total + jax.ops.segment_sum(plane_signal.astype(jnp.float32), plane_cells, num_segments=CELLS), None

    totals, _ = lax.scan(collect, jnp.zeros((CELLS, TICKS), jnp.float32), (signal, cell_map))
    return signal, totals * charge_scale
```

```python
import functools
import math

import jax
import jax.numpy as jnp
import ml_dtypes
import numpy as np
from jax import lax
from jax.experimental import pallas as pl
from jax.experimental.pallas import tpu as pltpu
from jax.sharding import PartitionSpec as P

TICKS = 2048
RESP_TAPS = 21
ROI_TICKS = 128
CELLS_OWN = 8
FREQS = 1024
HALO = 10
PAD = 16
LANES = 128
FTILES = FREQS // LANES
CHARGE_SCALE = 0.1
MESH = pl.DeviceIdType.MESH
CHUNKS = (256, 256, 128)
ROWS = 16


def build_table():
    frequency = np.arange(FREQS, dtype=np.int64)
    tick = np.arange(TICKS, dtype=np.int64)
    angle = ((tick[:, None] * frequency[None, :]) % TICKS).astype(np.float32) * np.float32(
        2.0 * math.pi / TICKS
    )
    cosine = np.cos(angle).astype(ml_dtypes.bfloat16).reshape(TICKS, FTILES, LANES)
    sine = (-np.sin(angle)).astype(ml_dtypes.bfloat16).reshape(TICKS, FTILES, LANES)
    return np.concatenate([cosine, sine], axis=2).reshape(TICKS, 2 * FREQS)


def windows(wires):
    chunks, outs, start = [], [], 0
    done = 0
    for size in CHUNKS:
        stop = start + size
        chunks.append((start, size))
        last = wires if stop == wires else stop - PAD
        outs.append((done, last - done))
        start, done = stop, last
    return chunks, outs


def kernel(
    n,
    x_ref,
    table_hbm,
    response_ref,
    wiener_ref,
    mask_ref,
    cells_ref,
    signal_ref,
    charge_ref,
    table,
    waves,
    turned,
    spec,
    coef,
    filtered,
    signal,
    selector,
    pair_out,
    pair_in,
    own_part,
    cell_out,
    cell_in,
    send_sem,
    recv_sem,
    local_sem,
    table_sem,
    halo_sem,
    pair_sem,
    cell_sem,
    out_sem,
):
    me = lax.axis_index("tick")
    side = lax.axis_index("wire")
    block, wires = x_ref.shape[1], x_ref.shape[2]
    cells = CELLS_OWN * n
    half = TICKS // 2
    chunks, outs = windows(wires)

    def place(start, size, unit):
        return pl.multiple_of(jnp.where(side == 1, start, wires - start - size), unit)

    table_copy = pltpu.make_async_copy(table_hbm, table, table_sem)
    table_copy.start()

    barrier = pltpu.get_barrier_semaphore()

    @pl.loop(1, n)
    def _(k):
        pl.semaphore_signal(
            barrier, inc=1, device_id={"tick": lax.rem(me + k, n)}, device_id_type=MESH
        )

    pl.semaphore_signal(barrier, inc=1, device_id={"wire": 1 - side}, device_id_type=MESH)
    pl.semaphore_wait(barrier, n)

    mine = pl.ds(pl.multiple_of(me * block, block), block)
    for c, (start, size) in enumerate(chunks):
        lanes = pl.ds(place(start, size, LANES), size)

        @pl.loop(1, n)
        def _(k):
            peer = lax.rem(me + k, n)
            pltpu.make_async_remote_copy(
                src_ref=x_ref.at[peer, :, lanes],
                dst_ref=waves.at[mine, lanes],
                send_sem=send_sem.at[c],
                recv_sem=recv_sem.at[c],
                device_id={"tick": peer},
                device_id_type=MESH,
            ).start()

    local_copy = pltpu.make_async_copy(x_ref.at[me], waves.at[mine, :], local_sem)
    local_copy.start()

    for j in range(FTILES):
        cols = slice(j * LANES, (j + 1) * LANES)
        gain = wiener_ref[:, cols] * (2.0 / TICKS)
        if j == 0:
            gain = jnp.where(lax.broadcasted_iota(jnp.int32, (1, LANES), 1) == 0, 0.5, 1.0) * gain
        real = response_ref[0, :, cols] * gain
        imag = response_ref[1, :, cols] * gain
        coef[j, 0, 0:RESP_TAPS, :] = real
        coef[j, 1, 0:RESP_TAPS, :] = real + imag
        coef[j, 2, 0:RESP_TAPS, :] = imag - real

    labels = lax.broadcasted_iota(jnp.int32, (cells, wires), 0)
    selector[...] = (cells_ref[...] == labels).astype(jnp.float32).astype(jnp.bfloat16)
    outer = pl.multiple_of(jnp.where(side == 1, PAD + wires, 0), PAD)
    for part in range(3):
        spec[part, :, pl.ds(outer, PAD), :] = jnp.zeros((FTILES, PAD, LANES), jnp.float32)

    def halo_copy():
        src = pl.multiple_of(jnp.where(side == 1, PAD, wires), PAD)
        dst = pl.multiple_of(jnp.where(side == 1, PAD + wires, 0), PAD)
        return pltpu.make_async_remote_copy(
            src_ref=spec.at[:, :, pl.ds(src, PAD), :],
            dst_ref=spec.at[:, :, pl.ds(dst, PAD), :],
            send_sem=halo_sem.at[0],
            recv_sem=halo_sem.at[1],
            device_id={"wire": 1 - side},
            device_id_type=MESH,
        )

    local_copy.wait()
    table_copy.wait()
    out_copies = []
    for c, ((start, size), (first, count)) in enumerate(zip(chunks, outs)):
        base = place(start, size, LANES)
        lanes = pl.ds(base, size)
        others = waves.at[pl.ds(0, (n - 1) * block), lanes]
        pltpu.make_async_copy(others, others, recv_sem.at[c]).wait()
        turned[0:size, :] = waves[:, lanes].T

        @pl.loop(0, FTILES)
        def _(j):
            cols = pl.ds(pl.multiple_of(j * 2 * LANES, 2 * LANES), 2 * LANES)
            product = jnp.dot(
                turned[0:size, :], table[:, cols], preferred_element_type=jnp.float32
            )
            real, imag = product[:, :LANES], product[:, LANES:]
            rows = pl.ds(pl.multiple_of(base + PAD, PAD), size)
            spec[0, j, rows, :] = real
            spec[1, j, rows, :] = imag
            spec[2, j, rows, :] = real + imag

        if c == 0:
            halo = halo_copy()
            halo.start()
            halo.wait()

        at = place(first, count, PAD)

        @pl.loop(0, FTILES)
        def _(j):
            @pl.loop(0, count // ROWS)
            def _(b):
                row = pl.multiple_of(at + b * ROWS, ROWS)
                acc_s = jnp.zeros((ROWS, LANES), jnp.float32)
                acc_i = jnp.zeros((ROWS, LANES), jnp.float32)
                acc_r = jnp.zeros((ROWS, LANES), jnp.float32)
                for d in range(RESP_TAPS):
                    rows = pl.ds(row + (PAD - HALO + d), ROWS)
                    acc_s = acc_s + coef[j, 0, d : d + 1, :] * spec[2, j, rows, :]
                    acc_i = acc_i + coef[j, 1, d : d + 1, :] * spec[1, j, rows, :]
                    acc_r = acc_r + coef[j, 2, d : d + 1, :] * spec[0, j, rows, :]
                col = pl.multiple_of(j * 2 * LANES, 2 * LANES)
                both = jnp.concatenate([acc_s - acc_i, acc_s + acc_r], axis=1)
                filtered[pl.ds(row, ROWS), pl.ds(col, 2 * LANES)] = both.astype(jnp.bfloat16)

        out_rows = pl.ds(at, count)
        roi = mask_ref[out_rows, :].astype(jnp.float32).astype(jnp.bfloat16)

        @pl.loop(0, TICKS // 256)
        def _(i):
            ticks = pl.ds(pl.multiple_of(i * 256, 256), 256)
            unmasked = lax.dot_general(
                filtered[out_rows, :],
                table[ticks, :],
                (((1,), (1,)), ((), ())),
                preferred_element_type=jnp.float32,
            )
            shape = (TICKS // ROI_TICKS, 256)
            spread = (
                lax.broadcasted_iota(jnp.int32, shape, 1) // ROI_TICKS + i * (256 // ROI_TICKS)
                == lax.broadcasted_iota(jnp.int32, shape, 0)
            ).astype(jnp.float32).astype(jnp.bfloat16)
            keep = jnp.dot(roi, spread, preferred_element_type=jnp.float32)
            signal[out_rows, ticks] = (unmasked * keep).astype(jnp.bfloat16)

        out_copy = pltpu.make_async_copy(
            signal.at[out_rows, :], signal_ref.at[out_rows, :], out_sem.at[c]
        )
        out_copy.start()
        out_copies.append(out_copy)

    def charge_of(which):
        lanes = pl.ds(pl.multiple_of(which * half, half), half)
        return jnp.dot(selector[...], signal[:, lanes], preferred_element_type=jnp.float32)

    pair_out[...] = charge_of(1 - side).astype(jnp.bfloat16)
    pair_copy = pltpu.make_async_remote_copy(
        src_ref=pair_out,
        dst_ref=pair_in,
        send_sem=pair_sem.at[0],
        recv_sem=pair_sem.at[1],
        device_id={"wire": 1 - side},
        device_id_type=MESH,
    )
    pair_copy.start()
    own_part[...] = charge_of(side)
    pair_copy.wait()
    quarter = half // 2

    total = (own_part[...] + pair_in[...].astype(jnp.float32)).reshape(n, CELLS_OWN, half)
    cell_out[...] = jnp.concatenate(
        [total[:, :, :quarter], total[:, :, quarter:]], axis=1
    ).astype(jnp.bfloat16)

    @pl.loop(1, n)
    def _(k):
        peer = lax.rem(me + k, n)
        pltpu.make_async_remote_copy(
            src_ref=cell_out.at[peer],
            dst_ref=cell_in.at[me],
            send_sem=cell_sem.at[0],
            recv_sem=cell_sem.at[1],
            device_id={"tick": peer},
            device_id_type=MESH,
        ).start()

    own_copy = pltpu.make_async_copy(cell_out.at[me], cell_in.at[me], local_sem)
    own_copy.start()
    own_copy.wait()
    arrived = cell_in.at[pl.ds(0, n - 1)]
    pltpu.make_async_copy(arrived, arrived, cell_sem.at[1]).wait()
    summed = jnp.sum(cell_in[...].astype(jnp.float32), axis=0) * CHARGE_SCALE
    charge_ref[:, 0:quarter] = summed[:CELLS_OWN]
    charge_ref[:, quarter:half] = summed[CELLS_OWN:]

    sent = cell_out.at[pl.ds(0, n - 1)]
    pltpu.make_async_copy(sent, sent, cell_sem.at[0]).wait()
    for c, (start, size) in enumerate(chunks):
        others = waves.at[pl.ds(0, (n - 1) * block), pl.ds(place(start, size, LANES), size)]
        pltpu.make_async_copy(others, others, send_sem.at[c]).wait()
    for out_copy in out_copies:
        out_copy.wait()


def on_device(trigger, response, wiener, roi_mask, cell_map):
    n = lax.axis_size("tick")
    wires = trigger.shape[2]
    cells = CELLS_OWN * n
    table = jnp.asarray(build_table())
    x = jnp.swapaxes(trigger, 0, 1)
    any_space = pl.BlockSpec(memory_space=pl.ANY)
    vmem = pl.BlockSpec(memory_space=pltpu.VMEM)
    bf16, f32 = jnp.bfloat16, jnp.float32
    half = TICKS // 2
    dma = pltpu.SemaphoreType.DMA
    signal, charge = pl.pallas_call(
        functools.partial(kernel, n),
        out_shape=(
            jax.ShapeDtypeStruct((wires, TICKS), bf16),
            jax.ShapeDtypeStruct((CELLS_OWN, half), f32),
        ),
        in_specs=[any_space, any_space, vmem, vmem, vmem, vmem],
        out_specs=(any_space, vmem),
        scratch_shapes=[
            pltpu.VMEM((TICKS, 2 * FREQS), bf16),
            pltpu.VMEM((TICKS, wires), bf16),
            pltpu.VMEM((max(CHUNKS), TICKS), bf16),
            pltpu.VMEM((3, FTILES, wires + 2 * PAD, LANES), f32),
            pltpu.VMEM((FTILES, 3, 24, LANES), f32),
            pltpu.VMEM((wires, 2 * FREQS), bf16),
            pltpu.VMEM((wires, TICKS), bf16),
            pltpu.VMEM((cells, wires), bf16),
            pltpu.VMEM((cells, half), bf16),
            pltpu.VMEM((cells, half), bf16),
            pltpu.VMEM((cells, half), f32),
            pltpu.VMEM((n, 16, half // 2), bf16),
            pltpu.VMEM((n, 16, half // 2), bf16),
            dma((len(CHUNKS),)),
            dma((len(CHUNKS),)),
            dma,
            dma,
            dma((2,)),
            dma((2,)),
            dma((2,)),
            dma((len(CHUNKS),)),
        ],
        compiler_params=pltpu.CompilerParams(
            collective_id=0, has_side_effects=True, vmem_limit_bytes=56 * 1024 * 1024
        ),
        cost_estimate=pl.CostEstimate(
            flops=4 * wires * TICKS * 2 * FREQS, bytes_accessed=20_000_000, transcendentals=0
        ),
    )(x, table, response, wiener[None], roi_mask[0], cell_map)
    return (signal[None], charge)


def solution(mesh):
    in_specs = (P("tick", None, "wire"), P(), P(), P("tick", "wire", None), P("tick", "wire"))
    out_specs = (P("tick", "wire", None), P("tick", "wire"))
    return jax.shard_map(
        on_device, mesh=mesh, in_specs=in_specs, out_specs=out_specs, check_vma=False
    )
```

```python
import functools
import math

import jax
import jax.numpy as jnp
import ml_dtypes
import numpy as np
from jax import lax
from jax.experimental import pallas as pl
from jax.experimental.pallas import tpu as pltpu
from jax.sharding import PartitionSpec as P

TICKS = 2048
RESP_TAPS = 21
ROI_TICKS = 128
CELLS_OWN = 8
FREQS = 1024
HALO = 10
PAD = 16
LANES = 128
FTILES = FREQS // LANES
CHARGE_SCALE = 0.1
MESH = pl.DeviceIdType.MESH
CHUNKS = (128, 128, 128, 128, 128)
AHEAD = 2
ROWS = 16
MOVES = 5


def build_table():
    order = np.arange(FREQS, dtype=np.int64).reshape(FREQS // 2, 2).T.reshape(-1)
    tick = np.arange(TICKS // 2, dtype=np.int64)
    angle = ((tick[:, None] * order[None, :]) % TICKS).astype(np.float32) * np.float32(
        2.0 * math.pi / TICKS
    )
    shape = (TICKS // 2, FTILES, LANES)
    cosine = np.cos(angle).astype(ml_dtypes.bfloat16).reshape(shape)
    sine = (-np.sin(angle)).astype(ml_dtypes.bfloat16).reshape(shape)
    return np.concatenate([cosine, sine], axis=2).reshape(TICKS // 2, 2 * FREQS)


def windows(wires):
    chunks, outs, start = [], [], 0
    done = 0
    for size in CHUNKS:
        stop = start + size
        chunks.append((start, size))
        last = wires if stop == wires else stop - PAD
        outs.append((done, last - done))
        start, done = stop, last
    return chunks, outs


def kernel(
    n,
    x_ref,
    table_hbm,
    back_hbm,
    response_ref,
    wiener_ref,
    mask_ref,
    cells_ref,
    signal_ref,
    charge_ref,
    table,
    back,
    roi,
    waves,
    turned,
    spec,
    coef,
    filtered,
    signal,
    selector,
    pair_out,
    pair_in,
    own_part,
    cell_out,
    cell_in,
    send_sem,
    recv_sem,
    local_sem,
    table_sem,
    back_sem,
    halo_sem,
    pair_sem,
    cell_sem,
    out_sem,
):
    me = lax.axis_index("tick")
    side = lax.axis_index("wire")
    block, wires = x_ref.shape[1], x_ref.shape[2]
    cells = CELLS_OWN * n
    half = TICKS // 2
    chunks, outs = windows(wires)

    def place(start, size, unit):
        return pl.multiple_of(jnp.where(side == 1, start, wires - start - size), unit)

    table_copy = pltpu.make_async_copy(table_hbm, table, table_sem)
    table_copy.start()
    back_copy = pltpu.make_async_copy(back_hbm, back, back_sem)
    back_copy.start()

    barrier = pltpu.get_barrier_semaphore()

    @pl.loop(1, n)
    def _(k):
        pl.semaphore_signal(
            barrier, inc=1, device_id={"tick": lax.rem(me + k, n)}, device_id_type=MESH
        )

    pl.semaphore_signal(barrier, inc=1, device_id={"wire": 1 - side}, device_id_type=MESH)
    pl.semaphore_wait(barrier, n)

    mine = pl.ds(pl.multiple_of(me * block, block), block)
    def send(c):
        start, size = chunks[c]
        lanes = pl.ds(place(start, size, LANES), size)

        @pl.loop(1, n)
        def _(k):
            peer = lax.rem(me + k, n)
            pltpu.make_async_remote_copy(
                src_ref=x_ref.at[peer, :, lanes],
                dst_ref=waves.at[mine, lanes],
                send_sem=send_sem.at[c],
                recv_sem=recv_sem.at[c],
                device_id={"tick": peer},
                device_id_type=MESH,
            ).start()

    for c in range(AHEAD):
        send(c)

    local_copy = pltpu.make_async_copy(x_ref.at[me], waves.at[mine, :], local_sem)
    local_copy.start()

    first_one = lax.broadcasted_iota(jnp.int32, (1, FREQS), 1) == 0
    gain = jnp.where(first_one, 0.5, 1.0) * wiener_ref[...] * (2.0 / TICKS)
    real = response_ref[:, 0, :] * gain
    imag = response_ref[:, 1, :] * gain

    @pl.loop(0, FTILES)
    def _(j):
        shape = (FREQS, LANES)
        column = lax.broadcasted_iota(jnp.int32, shape, 1) + lax.rem(j, FTILES // 2) * LANES
        wanted = 2 * column + j // (FTILES // 2)
        pick = (lax.broadcasted_iota(jnp.int32, shape, 0) == wanted).astype(jnp.float32)
        picked = functools.partial(
            jnp.dot, preferred_element_type=jnp.float32, precision=lax.Precision.HIGHEST
        )
        real_j, imag_j = picked(real, pick), picked(imag, pick)
        coef[j, 0, 0:RESP_TAPS, :] = real_j
        coef[j, 1, 0:RESP_TAPS, :] = real_j + imag_j
        coef[j, 2, 0:RESP_TAPS, :] = imag_j - real_j

    roi[...] = mask_ref[...].astype(jnp.float32).T
    labels = lax.broadcasted_iota(jnp.int32, (cells, wires), 0)
    selector[...] = (cells_ref[...] == labels).astype(jnp.float32).astype(jnp.bfloat16)
    outer = pl.multiple_of(jnp.where(side == 1, PAD + wires, 0), PAD)
    for part in range(3):
        spec[part, :, pl.ds(outer, PAD), :] = jnp.zeros((FTILES, PAD, LANES), jnp.float32)

    def halo_copy():
        src = pl.multiple_of(jnp.where(side == 1, PAD, wires), PAD)
        dst = pl.multiple_of(jnp.where(side == 1, PAD + wires, 0), PAD)
        return pltpu.make_async_remote_copy(
            src_ref=spec.at[:, :, pl.ds(src, PAD), :],
            dst_ref=spec.at[:, :, pl.ds(dst, PAD), :],
            send_sem=halo_sem.at[0],
            recv_sem=halo_sem.at[1],
            device_id={"wire": 1 - side},
            device_id_type=MESH,
        )

    local_copy.wait()
    table_copy.wait()
    back_copy.wait()
    out_copies = []
    for c, ((start, size), (first, count)) in enumerate(zip(chunks, outs)):
        base = place(start, size, LANES)
        lanes = pl.ds(base, size)
        others = waves.at[pl.ds(0, (n - 1) * block), lanes]
        pltpu.make_async_copy(others, others, recv_sem.at[c]).wait()
        if c + AHEAD < len(chunks):
            send(c + AHEAD)
        early, late = waves[0:half, lanes], waves[half:TICKS, lanes]
        turned[0, 0:size, :] = (early + late).T
        turned[1, 0:size, :] = (early - late).T

        @pl.loop(0, FTILES)
        def _(j):
            cols = pl.ds(pl.multiple_of(j * 2 * LANES, 2 * LANES), 2 * LANES)
            product = jnp.dot(
                turned[j // (FTILES // 2), 0:size, :], table[:, cols], preferred_element_type=jnp.float32
            )
            real, imag = product[:, :LANES], product[:, LANES:]
            rows = pl.ds(pl.multiple_of(base + PAD, PAD), size)
            spec[0, j, rows, :] = real
            spec[1, j, rows, :] = imag
            spec[2, j, rows, :] = real + imag

        if c == 0:
            halo = halo_copy()
            halo.start()
            halo.wait()

        at = place(first, count, PAD)

        @pl.loop(0, FTILES)
        def _(j):
            @pl.loop(0, count // ROWS)
            def _(b):
                row = pl.multiple_of(at + b * ROWS, ROWS)
                acc_s = jnp.zeros((ROWS, LANES), jnp.float32)
                acc_i = jnp.zeros((ROWS, LANES), jnp.float32)
                acc_r = jnp.zeros((ROWS, LANES), jnp.float32)
                for d in range(RESP_TAPS):
                    rows = pl.ds(row + (PAD - HALO + d), ROWS)
                    acc_s = acc_s + coef[j, 0, d : d + 1, :] * spec[2, j, rows, :]
                    acc_i = acc_i + coef[j, 1, d : d + 1, :] * spec[1, j, rows, :]
                    acc_r = acc_r + coef[j, 2, d : d + 1, :] * spec[0, j, rows, :]
                col = pl.multiple_of(j * 2 * LANES, 2 * LANES)
                both = jnp.concatenate([acc_s - acc_i, acc_s + acc_r], axis=1)
                filtered[pl.ds(row, ROWS), pl.ds(col, 2 * LANES)] = both.astype(jnp.bfloat16)

        out_rows = pl.ds(at, count)
        blocks = roi[out_rows, :]
        for i in range(half // 256):
            ticks = slice(i * 256, (i + 1) * 256)
            even = jnp.dot(
                filtered[out_rows, 0:FREQS],
                back[0:FREQS, ticks],
                preferred_element_type=jnp.float32,
            )
            odd = jnp.dot(
                filtered[out_rows, FREQS:],
                back[FREQS:, ticks],
                preferred_element_type=jnp.float32,
            )
            for base_tick, value in ((0, even + odd), (half, even - odd)):
                for part in range(2):
                    tick = base_tick + i * 256 + part * ROI_TICKS
                    at_block = tick // ROI_TICKS
                    keep = blocks[:, at_block : at_block + 1]
                    kept = value[:, part * ROI_TICKS : (part + 1) * ROI_TICKS] * keep
                    signal[out_rows, tick : tick + ROI_TICKS] = kept.astype(jnp.bfloat16)

        out_copy = pltpu.make_async_copy(
            signal.at[out_rows, :], signal_ref.at[out_rows, :], out_sem.at[c]
        )
        out_copy.start()
        out_copies.append(out_copy)

    def charge_of(which):
        lanes = pl.ds(pl.multiple_of(which * half, half), half)
        return jnp.dot(selector[...], signal[:, lanes], preferred_element_type=jnp.float32)

    pair_out[...] = charge_of(1 - side).astype(jnp.bfloat16)
    pair_copy = pltpu.make_async_remote_copy(
        src_ref=pair_out,
        dst_ref=pair_in,
        send_sem=pair_sem.at[0],
        recv_sem=pair_sem.at[1],
        device_id={"wire": 1 - side},
        device_id_type=MESH,
    )
    pair_copy.start()
    own_part[...] = charge_of(side)
    pair_copy.wait()
    quarter = half // 2

    total = (own_part[...] + pair_in[...].astype(jnp.float32)).reshape(n, CELLS_OWN, half)
    cell_out[...] = jnp.concatenate(
        [total[:, :, :quarter], total[:, :, quarter:]], axis=1
    ).astype(jnp.bfloat16)

    @pl.loop(1, n)
    def _(k):
        peer = lax.rem(me + k, n)
        pltpu.make_async_remote_copy(
            src_ref=cell_out.at[peer],
            dst_ref=cell_in.at[me],
            send_sem=cell_sem.at[0],
            recv_sem=cell_sem.at[1],
            device_id={"tick": peer},
            device_id_type=MESH,
        ).start()

    own_copy = pltpu.make_async_copy(cell_out.at[me], cell_in.at[me], local_sem)
    own_copy.start()
    own_copy.wait()
    arrived = cell_in.at[pl.ds(0, n - 1)]
    pltpu.make_async_copy(arrived, arrived, cell_sem.at[1]).wait()
    summed = jnp.sum(cell_in[...].astype(jnp.float32), axis=0) * CHARGE_SCALE
    charge_ref[:, 0:quarter] = summed[:CELLS_OWN]
    charge_ref[:, quarter:half] = summed[CELLS_OWN:]

    sent = cell_out.at[pl.ds(0, n - 1)]
    pltpu.make_async_copy(sent, sent, cell_sem.at[0]).wait()
    for c, (start, size) in enumerate(chunks):
        others = waves.at[pl.ds(0, (n - 1) * block), pl.ds(place(start, size, LANES), size)]
        pltpu.make_async_copy(others, others, send_sem.at[c]).wait()
    for out_copy in out_copies:
        out_copy.wait()


def hand_over(signal_in, charge_in, signal_out, charge_out):
    signal_out[...] = signal_in[...]

    @pl.when(pl.program_id(0) == 0)
    def _():
        charge_out[...] = charge_in[...]


def on_device(trigger, response, wiener, roi_mask, cell_map):
    n = lax.axis_size("tick")
    wires = trigger.shape[2]
    cells = CELLS_OWN * n
    table_np = build_table()
    x = jnp.swapaxes(trigger, 0, 1)
    any_space = pl.BlockSpec(memory_space=pl.ANY)
    vmem = pl.BlockSpec(memory_space=pltpu.VMEM)
    bf16, f32 = jnp.bfloat16, jnp.float32
    half = TICKS // 2
    dma = pltpu.SemaphoreType.DMA
    signal, charge = pl.pallas_call(
        functools.partial(kernel, n),
        out_shape=(
            jax.ShapeDtypeStruct((wires, TICKS), bf16),
            jax.ShapeDtypeStruct((CELLS_OWN, half), f32),
        ),
        in_specs=[any_space, any_space, any_space, vmem, vmem, vmem, vmem],
        out_specs=(any_space, vmem),
        scratch_shapes=[
            pltpu.VMEM((half, 2 * FREQS), bf16),
            pltpu.VMEM((2 * FREQS, half), bf16),
            pltpu.VMEM((wires, TICKS // ROI_TICKS), f32),
            pltpu.VMEM((TICKS, wires), bf16),
            pltpu.VMEM((2, max(CHUNKS), half), bf16),
            pltpu.VMEM((3, FTILES, wires + 2 * PAD, LANES), f32),
            pltpu.VMEM((FTILES, 3, 24, LANES), f32),
            pltpu.VMEM((wires, 2 * FREQS), bf16),
            pltpu.VMEM((wires, TICKS), bf16),
            pltpu.VMEM((cells, wires), bf16),
            pltpu.VMEM((cells, half), bf16),
            pltpu.VMEM((cells, half), bf16),
            pltpu.VMEM((cells, half), f32),
            pltpu.VMEM((n, 16, half // 2), bf16),
            pltpu.VMEM((n, 16, half // 2), bf16),
            dma((len(CHUNKS),)),
            dma((len(CHUNKS),)),
            dma,
            dma,
            dma,
            dma((2,)),
            dma((2,)),
            dma((2,)),
            dma((len(CHUNKS),)),
        ],
        compiler_params=pltpu.CompilerParams(
            collective_id=0, has_side_effects=True, vmem_limit_bytes=56 * 1024 * 1024
        ),
        cost_estimate=pl.CostEstimate(
            flops=4 * wires * TICKS * 2 * FREQS, bytes_accessed=20_000_000, transcendentals=0
        ),
    )(
        x,
        jnp.asarray(table_np),
        jnp.asarray(np.ascontiguousarray(table_np.T)),
        jnp.swapaxes(response, 0, 1),
        wiener[None],
        jnp.swapaxes(roi_mask[0], 0, 1),
        cell_map,
    )
    part = pl.BlockSpec((wires // MOVES, TICKS), lambda i: (i, 0))
    whole = pl.BlockSpec((CELLS_OWN, half), lambda i: (0, 0))
    signal, charge = pl.pallas_call(
        hand_over,
        out_shape=(
            jax.ShapeDtypeStruct(signal.shape, bf16),
            jax.ShapeDtypeStruct(charge.shape, f32),
        ),
        grid=(MOVES,),
        in_specs=[part, whole],
        out_specs=(part, whole),
    )(signal, charge)
    return (signal[None], charge)


def solution(mesh):
    in_specs = (P("tick", None, "wire"), P(), P(), P("tick", "wire", None), P("tick", "wire"))
    out_specs = (P("tick", "wire", None), P("tick", "wire"))
    return jax.shard_map(
        on_device, mesh=mesh, in_specs=in_specs, out_specs=out_specs, check_vma=False
    )
```
